32 devices in a mesh: seq: 8 (over z, y), head: 4 (over x, core).
Axes of the slice: x: 2, y: 2, z: 4, core: 2. Of those that a mesh axis runs over, the one named last changes fastest.
Arguments:
- tokens: bfloat16 [16384, 2048], P(('seq', 'head')), may hold values from -60 to 60
- query_index: int32 [1024], replicated, may hold values from 0 to 16383, as said below
- key_index: int32 [1024], replicated, may hold values from 0 to 16383, as said below
- light_query: bfloat16 [2048, 256], replicated, may hold values from -0.1875 to 0.1875
- light_key: bfloat16 [2048, 256], replicated, may hold values from -0.1875 to 0.1875
- light_value: bfloat16 [2048, 256], replicated, may hold values from -0.125 to 0.125
- light_out: bfloat16 [256, 2048], replicated, may hold values from -0.375 to 0.375
- heavy_query: bfloat16 [2048, 1024], P(None, 'head'), may hold values from -0.1875 to 0.1875
- heavy_key: bfloat16 [2048, 1024], P(None, 'head'), may hold values from -0.1875 to 0.1875
- heavy_value: bfloat16 [2048, 1024], P(None, 'head'), may hold values from -0.125 to 0.125
- heavy_out: bfloat16 [1024, 2048], P('head'), may hold values from -0.1875 to 0.1875
Outputs:
- layer_out: bfloat16 [16384, 2048], P(('seq', 'head'))
The draws below stay inside these ranges and needn't reach their ends.
Inputs may be any that keep to these rules, and one draw needn't show every extreme that they name: `query_index`: ascending and distinct token positions; at most 512 of them lie in one block of 2048 tokens starting at a multiple of 2048, and some block holds exactly 512. `key_index`: ascending and distinct token positions; at most 192 of them lie in one block of 2048 tokens starting at a multiple of 2048, and some block holds exactly 192.
All inputs are finite; a program needn't handle non-finite values.
Results may differ from the reference program's by a relative error of at most 0.02.
Values may be sent and summed in bfloat16 or wider, within the bound.
A program may use at most 128 MiB of HBM per device.

```python
import math
import jax
import jax.numpy as jnp
from jax import lax

D = 2048
HDIM = 64
LHEADS = 4
HHEADS = 16
RADIUS = 127
BLOCK = 2048
NBLK = 8
TOKENS = 16384
QROUTE = 1024
KROUTE = 1024
QCAP = 512
KCAP = 192


def routed_positions(key, total, most, low_weight, high_weight):
    first_key, second_key, third_key = jax.random.split(key, 3)
    block_ids = jnp.arange(NBLK, dtype=jnp.int32)
    hot_block = jax.random.randint(first_key, (), 0, NBLK, dtype=jnp.int32)
    is_hot = block_ids == hot_block
    weights_int = jax.random.randint(second_key, (NBLK,), low_weight, high_weight + 1, dtype=jnp.int32)
    weights_int = jnp.where(is_hot, 0, weights_int)
    remaining = total - most
    shares = remaining * weights_int // jnp.sum(weights_int)
    leftover = remaining - jnp.sum(shares)
    others_rank = jnp.cumsum(jnp.where(is_hot, 0, 1)) - 1
    shares = shares + jnp.where(~is_hot & (others_rank < leftover), 1, 0)
    counts = jnp.where(is_hot, most, shares).astype(jnp.int32)
    shuffled = jax.random.permutation(third_key, NBLK * BLOCK).astype(jnp.int32).reshape(NBLK, BLOCK)
    ranking = jnp.argsort(jnp.argsort(shuffled, axis=1, stable=True), axis=1, stable=True)
    chosen = (ranking < counts[:, None]).reshape(NBLK * BLOCK)
    return jnp.nonzero(chosen, size=total)[0].astype(jnp.int32)


def draw_query_index(key, part):
    return routed_positions(jax.random.fold_in(key, 11), QROUTE, QCAP, 2, 5)


def draw_key_index(key, part):
    return routed_positions(jax.random.fold_in(key, 23), KROUTE, KCAP, 4, 5)


def draw_tokens(key, part):
    first_key = jax.random.fold_in(jax.random.fold_in(key, 37), 0)
    entries = jax.random.truncated_normal(first_key, -5.0, 5.0, (TOKENS, D), jnp.float32)
    return entries.astype(jnp.bfloat16)


def block_levels(rng, extent, shards, least, top_value):
    level, own = 1.0, jax.random.fold_in(rng, 6)
    for dim, shards_of in shards:
        draws = jnp.exp(jax.random.uniform(jax.random.fold_in(own, dim), (shards_of,), jnp.float32, least / len(shards), top_value / len(shards)))
        level = level * jnp.repeat(draws, extent[dim] // shards_of).reshape([-1 if axis == dim else 1 for axis in range(len(extent))])
    return level


def noise(stream_key, shape, width, most, pieces=(), held_as=jnp.bfloat16):
    loudness = block_levels(stream_key, shape, pieces, -0.22, 0.18) if pieces else 1.0
    result = jax.random.normal(stream_key, shape, jnp.float32) * width * loudness
    return jnp.minimum(jnp.maximum(result, -most), most).astype(held_as)


def setup_inputs(seed: int = 0) -> dict:
    streams_of = jax.random.split(jax.random.key(seed), 12)
    tokens = draw_tokens(jax.random.fold_in(streams_of[11], 71), 0)
    query_index = draw_query_index(jax.random.fold_in(streams_of[11], 71), 0)
    key_index = draw_key_index(jax.random.fold_in(streams_of[11], 71), 0)
    light_query = noise(streams_of[3], (D, LHEADS * HDIM), (4 * D // 9) ** -0.5, 0.1875)
    light_key = noise(streams_of[4], (D, LHEADS * HDIM), (4 * D // 9) ** -0.5, 0.1875)
    light_value = noise(streams_of[5], (D, LHEADS * HDIM), D ** -0.5, 0.125)
    light_out = noise(streams_of[6], (LHEADS * HDIM, D), (LHEADS * HDIM) ** -0.5, 0.375)
    heavy_query = noise(streams_of[7], (D, HHEADS * HDIM), (4 * D // 9) ** -0.5, 0.1875, ((1, 4),))
    heavy_key = noise(streams_of[8], (D, HHEADS * HDIM), (4 * D // 9) ** -0.5, 0.1875, ((1, 4),))
    heavy_value = noise(streams_of[9], (D, HHEADS * HDIM), D ** -0.5, 0.125, ((1, 4),))
    heavy_out = noise(streams_of[10], (HHEADS * HDIM, D), (HHEADS * HDIM) ** -0.5, 0.1875, ((0, 4),))
    return dict(tokens=tokens, query_index=query_index, key_index=key_index, light_query=light_query, light_key=light_key, light_value=light_value, light_out=light_out, heavy_query=heavy_query, heavy_key=heavy_key, heavy_value=heavy_value, heavy_out=heavy_out)


def attend_rows(query_rows, key_rows, value_rows, allowed, head_count):
    row_count = query_rows.shape[0]
    key_count = key_rows.shape[0]
    head_dim = query_rows.shape[1] // head_count
    query_split = query_rows.astype(jnp.float32).reshape(row_count, head_count, head_dim)
    key_split = key_rows.astype(jnp.float32).reshape(key_count, head_count, head_dim)
    value_split = value_rows.astype(jnp.float32).reshape(key_count, head_count, head_dim)
    scores = jnp.einsum("qhd,khd->hqk", query_split, key_split) * (head_dim ** -0.5)
    scores = jnp.where(allowed[None], scores, -1e30)
    row_peak = jnp.max(scores, axis=2, keepdims=True)
    weights = jnp.where(allowed[None], jnp.exp(scores - row_peak), 0.0)
    row_total = jnp.sum(weights, axis=2)
    rounded = lax.optimization_barrier(weights.astype(jnp.bfloat16)).astype(jnp.float32)
    blended = jnp.einsum("hqk,khd->hqd", rounded, value_split) / row_total[:, :, None]
    blended = jnp.transpose(blended, (1, 0, 2)).reshape(row_count, head_count * head_dim)
    return blended.astype(jnp.bfloat16)


def project(rows_in, matrix):
    return jnp.dot(rows_in, matrix, preferred_element_type=jnp.float32).astype(jnp.bfloat16)


def reference(tokens, query_index, key_index, light_query, light_key, light_value, light_out, heavy_query, heavy_key, heavy_value, heavy_out):
    routed_q = project(tokens[query_index], heavy_query)
    routed_k = project(tokens[key_index], heavy_key)
    routed_v = project(tokens[key_index], heavy_value)
    every_key = jnp.ones((1, routed_k.shape[0]), dtype=bool)

    def one_head(head_number):
        start = head_number * HDIM
        return attend_rows(lax.dynamic_slice_in_dim(routed_q, start, HDIM, 1), lax.dynamic_slice_in_dim(routed_k, start, HDIM, 1), lax.dynamic_slice_in_dim(routed_v, start, HDIM, 1), every_key, 1)

    per_head = lax.map(one_head, jnp.arange(HHEADS, dtype=jnp.int32))
    heavy_mixed = jnp.transpose(per_head, (1, 0, 2)).reshape(routed_q.shape[0], HHEADS * HDIM)
    heavy_term = jnp.dot(heavy_mixed, heavy_out, preferred_element_type=jnp.float32)

    light_q_rows = project(tokens, light_query)
    light_k_rows = project(tokens, light_key)
    light_v_rows = project(tokens, light_value)
    margin = jnp.zeros((RADIUS, light_k_rows.shape[1]), jnp.bfloat16)
    key_padded = jnp.concatenate([margin, light_k_rows, margin], axis=0)
    value_padded = jnp.concatenate([margin, light_v_rows, margin], axis=0)
    span = math.gcd(TOKENS, 512)
    block_total = TOKENS // span

    def one_block(block_number):
        first = block_number * span
        query_rows = lax.dynamic_slice_in_dim(light_q_rows, first, span, 0)
        key_rows = lax.dynamic_slice_in_dim(key_padded, first, span + 2 * RADIUS, 0)
        value_rows = lax.dynamic_slice_in_dim(value_padded, first, span + 2 * RADIUS, 0)
        query_pos = first + jnp.arange(span, dtype=jnp.int32)
        key_pos = first - RADIUS + jnp.arange(span + 2 * RADIUS, dtype=jnp.int32)
        allowed = (jnp.abs(query_pos[:, None] - key_pos[None, :]) <= RADIUS) & (key_pos[None, :] >= 0) & (key_pos[None, :] < TOKENS)
        light_mixed = attend_rows(query_rows, key_rows, value_rows, allowed, LHEADS)
        light_term = jnp.dot(light_mixed, light_out, preferred_element_type=jnp.float32)
        slot = query_index - first
        slot = jnp.where((slot >= 0) & (slot < span), slot, span).astype(jnp.int32)
        heavy_part = jnp.zeros((span, D), jnp.float32).at[slot].add(heavy_term, mode="drop")
        return (light_term + heavy_part).astype(jnp.bfloat16)

    blocks = lax.map(one_block, jnp.arange(block_total, dtype=jnp.int32))
    return blocks.reshape(TOKENS, D)
```

```python
import functools

import jax
import jax.numpy as jnp
from jax import lax
from jax.experimental import pallas as pl
from jax.experimental.pallas import tpu as pltpu
from jax.sharding import PartitionSpec as P

HDIM = 64
LHEADS = 4
RADIUS = 127
HALO = 128
FLOOR = -1e30
VMEM_LIMIT = 48 * 1024 * 1024


def softmax_mix(q, k, v, allowed):
    scores = lax.dot_general(
        q, k, (((1,), (1,)), ((), ())), preferred_element_type=jnp.float32
    ) * (HDIM**-0.5)
    scores = jnp.where(allowed, scores, FLOOR)
    peak = jnp.max(scores, axis=1, keepdims=True)
    weights = jnp.exp(scores - peak)
    total = jnp.sum(weights, axis=1, keepdims=True)
    mixed = jnp.dot(weights.astype(jnp.bfloat16), v, preferred_element_type=jnp.float32)
    return (mixed / total).astype(jnp.bfloat16)


def light_kernel(total_len, first_ref, q_ref, kv_ref, o_ref):
    rows, width = q_ref.shape
    span = 3 * HALO
    for tile in range(rows // HALO):
        start = tile * HALO
        q_off = lax.broadcasted_iota(jnp.int32, (HALO, span), 0) + HALO
        k_off = lax.broadcasted_iota(jnp.int32, (HALO, span), 1)
        key_pos = first_ref[0] + (start - HALO) + k_off
        allowed = (
            (jnp.abs(q_off - k_off) <= RADIUS) & (key_pos >= 0) & (key_pos < total_len)
        )
        for head in range(width // HDIM):
            cols = slice(head * HDIM, (head + 1) * HDIM)
            vcols = slice(width + head * HDIM, width + (head + 1) * HDIM)
            o_ref[start : start + HALO, cols] = softmax_mix(
                q_ref[start : start + HALO, cols],
                kv_ref[start : start + span, cols],
                kv_ref[start : start + span, vcols],
                allowed,
            )


def light_attention(first, queries, pairs, total_len):
    return pl.pallas_call(
        functools.partial(light_kernel, total_len),
        out_shape=jax.ShapeDtypeStruct(queries.shape, jnp.bfloat16),
        in_specs=[
            pl.BlockSpec(memory_space=pltpu.SMEM),
            pl.BlockSpec(memory_space=pltpu.VMEM),
            pl.BlockSpec(memory_space=pltpu.VMEM),
        ],
        out_specs=pl.BlockSpec(memory_space=pltpu.VMEM),
        compiler_params=pltpu.CompilerParams(vmem_limit_bytes=VMEM_LIMIT),
        cost_estimate=pl.CostEstimate(
            flops=8 * queries.shape[0] * 3 * HALO * queries.shape[1],
            bytes_accessed=4 * queries.size * 2,
            transcendentals=queries.shape[0] * 3 * HALO * LHEADS,
        ),
    )(first, queries, pairs)


def heavy_kernel(q_ref, kv_ref, valid_ref, o_ref):
    width = q_ref.shape[1]
    allowed = valid_ref[...] > 0
    for head in range(width // HDIM):
        cols = slice(head * HDIM, (head + 1) * HDIM)
        vcols = slice(width + head * HDIM, width + (head + 1) * HDIM)
        o_ref[:, cols] = softmax_mix(q_ref[:, cols], kv_ref[:, cols], kv_ref[:, vcols], allowed)


def heavy_attention(queries, pairs, valid):
    rows, width = queries.shape
    keys = pairs.shape[0]
    tile = 128
    return pl.pallas_call(
        heavy_kernel,
        grid=(rows // tile,),
        out_shape=jax.ShapeDtypeStruct(queries.shape, jnp.bfloat16),
        in_specs=[
            pl.BlockSpec((tile, width), lambda i: (i, 0)),
            pl.BlockSpec((keys, 2 * width), lambda i: (0, 0)),
            pl.BlockSpec((1, keys), lambda i: (0, 0)),
        ],
        out_specs=pl.BlockSpec((tile, width), lambda i: (i, 0)),
        compiler_params=pltpu.CompilerParams(vmem_limit_bytes=VMEM_LIMIT),
    )(queries, pairs, valid)


def dot16(a, b):
    return jnp.dot(a, b, preferred_element_type=jnp.float32).astype(jnp.bfloat16)


def block_runs(index, seq_count, block_len, cap, seq_rank):
    starts = jnp.arange(seq_count, dtype=jnp.int32) * block_len
    firsts = jnp.sum((index[None, :] < starts[:, None]).astype(jnp.int32), axis=1)
    ends = jnp.sum((index[None, :] < starts[:, None] + block_len).astype(jnp.int32), axis=1)
    counts = ends - firsts
    padded = jnp.concatenate([index, jnp.zeros((cap,), jnp.int32)])
    run = lax.dynamic_slice_in_dim(padded, firsts[seq_rank], cap, 0)
    valid = jnp.arange(cap, dtype=jnp.int32) < counts[seq_rank]
    place = jnp.where(valid, run - seq_rank * block_len, -1)
    return place, counts


def shards(
    tokens,
    query_index,
    key_index,
    light_query,
    light_key,
    light_value,
    light_out,
    heavy_query,
    heavy_key,
    heavy_value,
    heavy_out,
):
    row_count = tokens.shape[0]
    group_size = lax.axis_size("head")
    seq_count = lax.axis_size("seq")
    block_len = row_count * group_size
    seq_rank = lax.axis_index("seq")
    head_rank = lax.axis_index("head")
    my_first = (seq_rank * group_size + head_rank) * row_count
    total_len = block_len * seq_count
    query_cap = block_len // 4
    key_cap = 3 * block_len // 32
    light_width = light_query.shape[1]
    heavy_width = heavy_query.shape[1]

    block_rows = lax.all_gather(tokens, "head", axis=0, tiled=True)
    heavy_out_all = lax.all_gather(heavy_out, "head", axis=0, tiled=True)

    light_all = dot16(tokens, jnp.concatenate([light_query, light_key, light_value], axis=1))
    light_pair = light_all[:, light_width:]
    count = seq_count * group_size
    forward = [(i, i + 1) for i in range(count - 1)]
    backward = [(i + 1, i) for i in range(count - 1)]
    low = lax.ppermute(light_pair[row_count - HALO :], ("seq", "head"), forward)
    high = lax.ppermute(light_pair[:HALO], ("seq", "head"), backward)
    padded = jnp.concatenate([low, light_pair, high], axis=0)
    light_mixed = light_attention(
        my_first.reshape(1), light_all[:, :light_width], padded, total_len
    )

    query_place, _ = block_runs(query_index, seq_count, block_len, query_cap, seq_rank)
    key_place, key_counts = block_runs(key_index, seq_count, block_len, key_cap, seq_rank)
    block_ids = jnp.arange(block_len, dtype=jnp.int32)
    query_pick = (query_place[:, None] == block_ids[None, :]).astype(jnp.bfloat16)
    key_pick = (key_place[:, None] == block_ids[None, :]).astype(jnp.bfloat16)
    local_ids = head_rank * row_count + jnp.arange(row_count, dtype=jnp.int32)
    place_back = (local_ids[:, None] == query_place[None, :]).astype(jnp.bfloat16)
    valid = (jnp.arange(key_cap, dtype=jnp.int32)[None, :] < key_counts[:, None]).astype(
        jnp.int32
    ).reshape(1, seq_count * key_cap)

    projected = dot16(block_rows, jnp.concatenate([heavy_key, heavy_value, heavy_query], axis=1))
    routed_pair = dot16(key_pick, projected[:, : 2 * heavy_width])
    every_pair = lax.all_gather(routed_pair, "seq", axis=0, tiled=True)
    routed_q = dot16(query_pick, projected[:, 2 * heavy_width :])
    mixed = heavy_attention(routed_q, every_pair, valid)
    every_mixed = lax.all_gather(mixed, "head", axis=1, tiled=True)
    heavy_mixed = dot16(place_back, every_mixed)
    return dot16(
        jnp.concatenate([light_mixed, heavy_mixed], axis=1),
        jnp.concatenate([light_out, heavy_out_all], axis=0),
    )


def solution(mesh):
    placed = (
        P(("seq", "head"), None),
        P(),
        P(),
        P(),
        P(),
        P(),
        P(),
        P(None, "head"),
        P(None, "head"),
        P(None, "head"),
        P("head", None),
    )
    return jax.shard_map(
        shards, mesh=mesh, in_specs=placed, out_specs=P(("seq", "head"), None), check_vma=False
    )
```

```python
import functools

import jax
import jax.numpy as jnp
from jax import lax
from jax.experimental import pallas as pl
from jax.experimental.pallas import tpu as pltpu
from jax.sharding import PartitionSpec as P

HDIM = 64
RADIUS = 127
HALO = 128
TILE = 128
FLOOR = -1e30
VMEM_LIMIT = 60 * 1024 * 1024
MESH = pl.DeviceIdType.MESH


def dot32(a, b):
    return jnp.dot(a, b, preferred_element_type=jnp.float32)


def dot16(a, b):
    return dot32(a, b).astype(jnp.bfloat16)


def softmax_mix(q, k, v, allowed):
    scores = lax.dot_general(
        q, k, (((1,), (1,)), ((), ())), preferred_element_type=jnp.float32
    ) * (HDIM**-0.5)
    scores = jnp.where(allowed, scores, FLOOR)
    peak = jnp.max(scores, axis=1, keepdims=True)
    weights = jnp.exp(scores - peak)
    total = jnp.sum(weights, axis=1, keepdims=True)
    mixed = dot32(weights.astype(jnp.bfloat16), v)
    return (mixed / total).astype(jnp.bfloat16)


def slot_places(index_ref, cap, first_token):
    total = index_ref.shape[1]
    piece = min(total, 1024)
    before = jnp.zeros((1, 1), jnp.int32)
    for start in range(0, total, piece):
        part = index_ref[:, start : start + piece]
        before += jnp.sum((part < first_token).astype(jnp.int32), axis=1, keepdims=True)
    place = jnp.zeros((cap, 1), jnp.int32)
    for start in range(0, total, piece):
        part = index_ref[:, start : start + piece]
        rank = lax.broadcasted_iota(jnp.int32, (cap, piece), 1) + (start - before)
        slot = lax.broadcasted_iota(jnp.int32, (cap, piece), 0)
        place += jnp.sum(jnp.where(rank == slot, part + 1, 0), axis=1, keepdims=True)
    return place - 1 - first_token


def key_mask(index_ref, seq_count, cap, block_len):
    position = lax.broadcasted_iota(jnp.int32, (1, seq_count * cap), 1)
    index = index_ref[...]
    mask = jnp.zeros((1, seq_count * cap), jnp.int32)
    for block in range(seq_count):
        inside = (index >= block * block_len) & (index < (block + 1) * block_len)
        count = jnp.sum(inside.astype(jnp.int32), axis=1, keepdims=True)
        hit = (position >= block * cap) & (position < block * cap + count)
        mask = mask | hit.astype(jnp.int32)
    return mask


def kernel(
    seq_count,
    group,
    tok,
    qi,
    ki,
    lq,
    lk,
    lv,
    lo,
    hq,
    hk,
    hv,
    ho,
    out,
    got_tok,
    place_ref,
    mask_ref,
    pick,
    pick_x,
    pick_core,
    light_q,
    light_kv,
    light_mix,
    pairs,
    queries,
    mix,
    walls,
    placed,
    send,
    recv,
):
    rows, width = tok.shape
    half = width // 2
    block_len = rows * group
    total_len = block_len * seq_count
    query_cap = queries.shape[0]
    key_cap = pairs.shape[1]
    hw = hq.shape[1]
    lw = lq.shape[1]
    zs = seq_count // 2
    s, h = lax.axis_index("seq"), lax.axis_index("head")
    x, c = h // 2, h % 2
    z, y = s // 2, s % 2
    core = (s, x * 2 + 1 - c)
    xp = (s, (1 - x) * 2 + c)
    yp = (z * 2 + 1 - y, h)
    zp = [None] + [(((z + d) % zs) * 2 + y, h) for d in range(1, zs)]
    flat, count = s * group + h, seq_count * group
    up, down = (flat + 1) % count, (flat + count - 1) % count
    above, below = (up // group, up % group), (down // group, down % group)
    partners = [core, xp, yp, above, below] + zp[1:]

    barrier = pltpu.get_barrier_semaphore()
    for device in partners:
        pl.semaphore_signal(barrier, inc=1, device_id=device, device_id_type=MESH)
    pl.semaphore_wait(barrier, len(partners))

    used = [0]
    begun = []

    def remote(src, dst, device):
        number = used[0]
        used[0] += 1
        copy = pltpu.make_async_remote_copy(
            src_ref=src,
            dst_ref=dst,
            send_sem=send.at[number],
            recv_sem=recv.at[number],
            device_id=device,
            device_id_type=MESH,
        )
        begun.append(copy)
        return copy

    mine = pl.multiple_of(c * half, half)
    other = pl.multiple_of((1 - c) * half, half)
    tok_copy = remote(tok.at[:, pl.ds(other, half)], got_tok, core)
    tok_copy.start()

    first_token = s * block_len
    place_ref[:key_cap] = slot_places(ki, key_cap, first_token)
    place_ref[key_cap:] = slot_places(qi, query_cap, first_token)
    mask_ref[...] = key_mask(ki, seq_count, key_cap, block_len)

    def chosen(start, size, owner):
        ids = lax.broadcasted_iota(jnp.int32, (size, rows), 1) + owner * rows
        hit = place_ref[start : start + size] == ids
        return hit.astype(jnp.float32).astype(jnp.bfloat16)

    def choose(start, size):
        pick[start : start + size] = (
            dot32(chosen(start, size, h), tok[:, pl.ds(mine, half)])
            + dot32(chosen(start, size, core[1]), got_tok[...])
        ).astype(jnp.bfloat16)

    tok_copy.wait_recv()
    choose(0, key_cap)
    span = pl.ds(0, key_cap)
    key_x = remote(pick.at[span], pick_x.at[span], xp)
    key_x.start()
    wall_core = remote(ho, walls.at[0], core)
    wall_core.start()

    spans = [(key_cap + i * TILE, TILE) for i in range(query_cap // TILE)]
    for start, size in spans:
        choose(start, size)

    def light_project(tile, carry):
        at = pl.multiple_of(tile * TILE, TILE)
        part = tok[pl.ds(at, TILE)]
        light_q[pl.ds(at, TILE)] = dot16(part, lq[...])
        light_kv[pl.ds(at + HALO, TILE), :lw] = dot16(part, lk[...])
        light_kv[pl.ds(at + HALO, TILE), lw:] = dot16(part, lv[...])
        return carry

    lax.fori_loop(0, rows // TILE, light_project, 0)
    to_above = remote(light_kv.at[pl.ds(rows, HALO)], light_kv.at[pl.ds(0, HALO)], above)
    to_above.start()
    to_below = remote(
        light_kv.at[pl.ds(HALO, HALO)], light_kv.at[pl.ds(rows + HALO, HALO)], below
    )
    to_below.start()

    key_x.wait()
    part_rows = ho.shape[0] // 2
    wall_part = pl.ds(pl.multiple_of(y * part_rows, part_rows), part_rows)
    wall_rest = pl.ds(pl.multiple_of((1 - y) * part_rows, part_rows), part_rows)
    wall_x = remote(ho.at[wall_part], walls.at[1, wall_part], xp)
    wall_x.start()

    def join(start, size):
        rows_here = pl.ds(start, size)
        pick[rows_here] = pick[rows_here] + pick_x[rows_here]
        copy = remote(pick.at[rows_here], pick_core.at[rows_here], core)
        copy.start()
        return copy

    def project(start, size, matrix):
        return (
            dot32(pick[start : start + size], matrix[pl.ds(mine, half)])
            + dot32(pick_core[start : start + size], matrix[pl.ds(other, half)])
        ).astype(jnp.bfloat16)

    key_core = join(0, key_cap)
    query_x = []
    for start, size in spans:
        copy = remote(pick.at[pl.ds(start, size)], pick_x.at[pl.ds(start, size)], xp)
        copy.start()
        query_x.append(copy)
    key_core.wait_recv()
    pairs[s, :, :hw] = project(0, key_cap, hk)
    pairs[s, :, hw:] = project(0, key_cap, hv)
    pair_z = [None]
    for d in range(1, zs):
        copy = remote(pairs.at[s], pairs.at[s], zp[d])
        copy.start()
        pair_z.append(copy)
    pair_y = [remote(pairs.at[s], pairs.at[s], yp)]
    pair_y[0].start()

    to_above.wait_recv()
    to_below.wait_recv()
    reach = 3 * HALO
    q_off = lax.broadcasted_iota(jnp.int32, (HALO, reach), 0) + HALO
    k_off = lax.broadcasted_iota(jnp.int32, (HALO, reach), 1)
    near = jnp.abs(q_off - k_off) <= RADIUS

    def light_tile(tile, carry):
        at = pl.multiple_of(tile * HALO, HALO)
        key_pos = flat * rows + (at - HALO) + k_off
        allowed = near & (key_pos >= 0) & (key_pos < total_len)
        for head in range(lw // HDIM):
            lo_col, hi_col = head * HDIM, (head + 1) * HDIM
            light_mix[pl.ds(at, HALO), lo_col:hi_col] = softmax_mix(
                light_q[pl.ds(at, HALO), lo_col:hi_col],
                light_kv[pl.ds(at, reach), lo_col:hi_col],
                light_kv[pl.ds(at, reach), lw + lo_col : lw + hi_col],
                allowed,
            )
        return carry

    lax.fori_loop(0, rows // HALO, light_tile, 0)

    for d in range(1, zs):
        pair_z[d].wait_recv()
        slot = ((z + zs - d) % zs) * 2 + y
        copy = remote(pairs.at[slot], pairs.at[slot], yp)
        copy.start()
        pair_y.append(copy)

    wall_x.wait_recv()
    wall_y = remote(walls.at[1, wall_part], walls.at[1, wall_part], yp)
    wall_y.start()
    wall_core_a = remote(walls.at[1, wall_part], walls.at[2, wall_part], core)
    wall_core_a.start()

    query_core = []
    for i, (start, size) in enumerate(spans):
        query_x[i].wait()
        query_core.append(join(start, size))
    for copy in pair_y:
        copy.wait_recv()

    keys = seq_count * key_cap
    step = TILE if keys <= 2048 else 32
    mix_x, mix_core, mix_far = [], [], []
    for i, (start, size) in enumerate(spans):
        at = start - key_cap
        query_core[i].wait_recv()
        queries[at : at + size] = project(start, size, hq)

        def heavy_tile(tile, carry):
            here = pl.multiple_of(at + tile * step, step)
            for head in range(hw // HDIM):
                lo_col, hi_col = head * HDIM, (head + 1) * HDIM
                mix[0, pl.ds(here, step), lo_col:hi_col] = softmax_mix(
                    queries[pl.ds(here, step), lo_col:hi_col],
                    pairs[:, :, lo_col:hi_col].reshape(keys, HDIM),
                    pairs[:, :, hw + lo_col : hw + hi_col].reshape(keys, HDIM),
                    mask_ref[...] > 0,
                )
            return carry

        lax.fori_loop(0, size // step, heavy_tile, 0)
        here = pl.ds(at, size)
        mix_x.append(remote(mix.at[0, here], mix.at[2, here], xp))
        mix_x[-1].start()
        mix_core.append(remote(mix.at[0, here], mix.at[1, here], core))
        mix_core[-1].start()
        if i == 0:
            wall_y.wait_recv()
            wall_core_b = remote(walls.at[1, wall_rest], walls.at[2, wall_rest], core)
            wall_core_b.start()
        else:
            mix_x[i - 1].wait_recv()
            before = pl.ds(at - TILE, TILE)
            mix_far.append(remote(mix.at[2, before], mix.at[3, before], core))
            mix_far[-1].start()
    mix_x[-1].wait_recv()
    last = pl.ds(query_cap - TILE, TILE)
    mix_far.append(remote(mix.at[2, last], mix.at[3, last], core))
    mix_far[-1].start()

    def back(part):
        pick_t = chosen(key_cap, query_cap, h)
        placed[part] = lax.dot_general(
            pick_t, mix[part], (((0,), (0,)), ((), ())), preferred_element_type=jnp.float32
        ).astype(jnp.bfloat16)

    back(0)
    for copy in mix_core:
        copy.wait_recv()
    back(1)
    back(2)
    for copy in mix_far:
        copy.wait_recv()
    back(3)
    wall_core.wait_recv()
    wall_core_a.wait_recv()
    wall_core_b.wait_recv()

    def finish(tile, carry):
        here = pl.ds(pl.multiple_of(tile * TILE, TILE), TILE)
        out[here] = (
            dot32(light_mix[here], lo[...])
            + dot32(placed[0, here], ho[...])
            + dot32(placed[1, here], walls[0])
            + dot32(placed[2, here], walls[1])
            + dot32(placed[3, here], walls[2])
        ).astype(jnp.bfloat16)
        return carry

    lax.fori_loop(0, rows // TILE, finish, 0)

    waited = [key_x] + query_x
    for copy in begun:
        if not any(copy is done for done in waited):
            copy.wait_send()


def shards(tokens, query_index, key_index, *weights):
    seq_count, group = lax.axis_size("seq"), lax.axis_size("head")
    rows, width = tokens.shape
    lw, hw = weights[0].shape[1], weights[4].shape[1]
    block_len = rows * group
    query_cap, key_cap = block_len // 4, 3 * block_len // 32
    slots = query_cap + key_cap
    copies = 8 + 2 * (seq_count // 2) + 5 * (query_cap // TILE) + 8
    bf16 = jnp.bfloat16
    return pl.pallas_call(
        functools.partial(kernel, seq_count, group),
        out_shape=jax.ShapeDtypeStruct(tokens.shape, bf16),
        in_specs=[pl.BlockSpec(memory_space=pltpu.VMEM)] * 11,
        out_specs=pl.BlockSpec(memory_space=pltpu.VMEM),
        scratch_shapes=[
            pltpu.VMEM((rows, width // 2), bf16),
            pltpu.VMEM((slots, 1), jnp.int32),
            pltpu.VMEM((1, seq_count * key_cap), jnp.int32),
            pltpu.VMEM((slots, width // 2), bf16),
            pltpu.VMEM((slots, width // 2), bf16),
            pltpu.VMEM((slots, width // 2), bf16),
            pltpu.VMEM((rows, lw), bf16),
            pltpu.VMEM((rows + 2 * HALO, 2 * lw), bf16),
            pltpu.VMEM((rows, lw), bf16),
            pltpu.VMEM((seq_count, key_cap, 2 * hw), bf16),
            pltpu.VMEM((query_cap, hw), bf16),
            pltpu.VMEM((4, query_cap, hw), bf16),
            pltpu.VMEM((3,) + weights[7].shape, bf16),
            pltpu.VMEM((4, rows, hw), bf16),
            pltpu.SemaphoreType.DMA((copies,)),
            pltpu.SemaphoreType.DMA((copies,)),
        ],
        compiler_params=pltpu.CompilerParams(
            collective_id=0, has_side_effects=True, vmem_limit_bytes=VMEM_LIMIT
        ),
    )(tokens, query_index.reshape(1, -1), key_index.reshape(1, -1), *weights)


def solution(mesh):
    placed = (
        P(("seq", "head"), None),
        P(),
        P(),
        P(),
        P(),
        P(),
        P(),
        P(None, "head"),
        P(None, "head"),
        P(None, "head"),
        P("head", None),
    )
    return jax.shard_map(
        shards, mesh=mesh, in_specs=placed, out_specs=P(("seq", "head"), None), check_vma=False
    )
```

```python
import functools

import jax
import jax.numpy as jnp
from jax import lax
from jax.experimental import pallas as pl
from jax.experimental.pallas import tpu as pltpu
from jax.sharding import PartitionSpec as P

HDIM = 64
RADIUS = 127
HALO = 128
TILE = 128
FLOOR = -1e30
VMEM_LIMIT = 60 * 1024 * 1024
MESH = pl.DeviceIdType.MESH


def dot32(a, b):
    return jnp.dot(a, b, preferred_element_type=jnp.float32)


def dot16(a, b):
    return dot32(a, b).astype(jnp.bfloat16)


def softmax_mix(q, k, v, bias):
    scores = lax.dot_general(
        q, k, (((1,), (1,)), ((), ())), preferred_element_type=jnp.float32
    ) + bias
    peak = jnp.max(scores, axis=1, keepdims=True)
    weights = jnp.exp(scores - peak)
    total = jnp.sum(weights, axis=1, keepdims=True)
    mixed = dot32(weights.astype(jnp.bfloat16), v)
    return (mixed / total).astype(jnp.bfloat16)


def slot_places(index_ref, cap, first_token):
    total = index_ref.shape[1]
    piece = min(total, 1024)
    before = jnp.zeros((1, 1), jnp.int32)
    for start in range(0, total, piece):
        part = index_ref[:, start : start + piece]
        before += jnp.sum((part < first_token).astype(jnp.int32), axis=1, keepdims=True)
    place = jnp.zeros((cap, 1), jnp.int32)
    for start in range(0, total, piece):
        part = index_ref[:, start : start + piece]
        rank = lax.broadcasted_iota(jnp.int32, (cap, piece), 1) + (start - before)
        slot = lax.broadcasted_iota(jnp.int32, (cap, piece), 0)
        place += jnp.sum(jnp.where(rank == slot, part + 1, 0), axis=1, keepdims=True)
    return place - 1 - first_token


def key_mask(index_ref, seq_count, cap, block_len):
    position = lax.broadcasted_iota(jnp.int32, (1, seq_count * cap), 1)
    index = index_ref[...]
    mask = jnp.zeros((1, seq_count * cap), jnp.int32)
    for block in range(seq_count):
        inside = (index >= block * block_len) & (index < (block + 1) * block_len)
        count = jnp.sum(inside.astype(jnp.int32), axis=1, keepdims=True)
        hit = (position >= block * cap) & (position < block * cap + count)
        mask = mask | hit.astype(jnp.int32)
    return jnp.where(mask > 0, 0.0, FLOOR)


def kernel(
    seq_count,
    group,
    tok,
    qi,
    ki,
    *refs,
):
    far, out, near_refs = refs[:8], refs[8], refs[9:17]
    lq, lk, lv, lo, hq, hk, hv, ho = near_refs
    (
        got_tok,
        place_ref,
        mask_ref,
        pick,
        pick_x,
        pick_core,
        light_q,
        light_kv,
        light_mix,
        pairs,
        queries,
        mix,
        walls,
        placed,
        load,
        send,
        recv,
    ) = refs[17:]
    loads = [
        pltpu.make_async_copy(a, b, load.at[i]) for i, (a, b) in enumerate(zip(far, near_refs))
    ]
    rows, width = tok.shape
    half = width // 2
    block_len = rows * group
    total_len = block_len * seq_count
    query_cap = queries.shape[0]
    key_cap = pairs.shape[1]
    hw = hq.shape[1]
    lw = lq.shape[1]
    zs = seq_count // 2
    s, h = lax.axis_index("seq"), lax.axis_index("head")
    x, c = h // 2, h % 2
    z, y = s // 2, s % 2
    core = (s, x * 2 + 1 - c)
    xp = (s, (1 - x) * 2 + c)
    yp = (z * 2 + 1 - y, h)
    zp = [None] + [(((z + d) % zs) * 2 + y, h) for d in range(1, zs)]
    flat, count = s * group + h, seq_count * group
    up, down = (flat + 1) % count, (flat + count - 1) % count
    above, below = (up // group, up % group), (down // group, down % group)
    partners = [core, xp, yp, above, below] + zp[1:]

    barrier = pltpu.get_barrier_semaphore()
    for device in partners:
        pl.semaphore_signal(barrier, inc=1, device_id=device, device_id_type=MESH)
    pl.semaphore_wait(barrier, len(partners))

    used = [0]
    begun = []

    def remote(src, dst, device):
        number = used[0]
        used[0] += 1
        copy = pltpu.make_async_remote_copy(
            src_ref=src,
            dst_ref=dst,
            send_sem=send.at[number],
            recv_sem=recv.at[number],
            device_id=device,
            device_id_type=MESH,
        )
        begun.append(copy)
        return copy

    mine = pl.multiple_of(c * half, half)
    other = pl.multiple_of((1 - c) * half, half)
    tok_copy = remote(tok.at[:, pl.ds(other, half)], got_tok, core)
    tok_copy.start()
    for i in (0, 1, 2, 5, 6, 4, 7, 3):
        loads[i].start()

    first_token = s * block_len
    place_ref[:key_cap] = slot_places(ki, key_cap, first_token)
    place_ref[key_cap:] = slot_places(qi, query_cap, first_token)
    mask_ref[...] = key_mask(ki, seq_count, key_cap, block_len)

    def chosen(start, size, owner):
        ids = lax.broadcasted_iota(jnp.int32, (size, rows), 1) + owner * rows
        hit = place_ref[start : start + size] == ids
        return hit.astype(jnp.float32).astype(jnp.bfloat16)

    def choose(start, size):
        pick[start : start + size] = (
            dot32(chosen(start, size, h), tok[:, pl.ds(mine, half)])
            + dot32(chosen(start, size, core[1]), got_tok[...])
        ).astype(jnp.bfloat16)

    tok_copy.wait_recv()
    choose(0, key_cap)
    span = pl.ds(0, key_cap)
    key_x = remote(pick.at[span], pick_x.at[span], xp)
    key_x.start()

    spans = [(key_cap + i * TILE, TILE) for i in range(query_cap // TILE)]
    for start, size in spans:
        choose(start, size)

    scale = jnp.asarray(HDIM**-0.5, jnp.bfloat16)
    for i in (0, 1, 2):
        loads[i].wait()

    def light_project(tile, carry):
        at = pl.multiple_of(tile * TILE, TILE)
        part = tok[pl.ds(at, TILE)]
        light_q[pl.ds(at, TILE)] = (dot32(part, lq[...]).astype(jnp.bfloat16)) * scale
        light_kv[pl.ds(at + HALO, TILE), :lw] = dot16(part, lk[...])
        light_kv[pl.ds(at + HALO, TILE), lw:] = dot16(part, lv[...])
        return carry

    lax.fori_loop(0, rows // TILE, light_project, 0)
    to_above = remote(light_kv.at[pl.ds(rows, HALO)], light_kv.at[pl.ds(0, HALO)], above)
    to_above.start()
    to_below = remote(
        light_kv.at[pl.ds(HALO, HALO)], light_kv.at[pl.ds(rows + HALO, HALO)], below
    )
    to_below.start()

    key_x.wait()
    piece = ho.shape[0] // 4
    ours = [pl.ds(pl.multiple_of((y * 2 + i) * piece, piece), piece) for i in range(2)]
    theirs = [pl.ds(pl.multiple_of((2 - y * 2 + i) * piece, piece), piece) for i in range(2)]

    def join(start, size):
        rows_here = pl.ds(start, size)
        pick_x[rows_here] = pick[rows_here] + pick_x[rows_here]
        copy = remote(pick_x.at[rows_here], pick_core.at[rows_here], core)
        copy.start()
        return copy

    def project(start, size, matrix):
        return (
            dot32(pick_x[start : start + size], matrix[pl.ds(mine, half)])
            + dot32(pick_core[start : start + size], matrix[pl.ds(other, half)])
        ).astype(jnp.bfloat16)

    query_x = [
        remote(pick.at[pl.ds(start, size)], pick_x.at[pl.ds(start, size)], xp)
        for start, size in spans
    ]
    sent = [0]

    def send_query():
        if sent[0] < len(query_x):
            if sent[0] >= 2:
                query_x[sent[0] - 2].wait_send()
            query_x[sent[0]].start()
            sent[0] += 1

    key_core = join(0, key_cap)
    send_query()
    send_query()
    loads[5].wait()
    loads[6].wait()
    key_core.wait_recv()
    pairs[s, :, :hw] = project(0, key_cap, hk)
    pairs[s, :, hw:] = project(0, key_cap, hv)
    order = sorted(range(1, zs), key=lambda d: min(d, zs - d))
    pair_z = [remote(pairs.at[s], pairs.at[s], zp[d]) for d in order]
    pair_z[0].start()
    pair_y = [remote(pairs.at[s], pairs.at[s], yp)]
    pair_y[0].start()
    loads[7].wait()
    wall_core = remote(ho, walls.at[0], core)
    wall_core.start()

    def forward_pair(number):
        pair_z[number].wait()
        if number + 1 < len(pair_z):
            pair_z[number + 1].start()
        slot = ((z + zs - order[number]) % zs) * 2 + y
        copy = remote(pairs.at[slot], pairs.at[slot], yp)
        copy.start()
        pair_y.append(copy)

    to_above.wait_recv()
    to_below.wait_recv()
    reach = 3 * HALO
    q_off = lax.broadcasted_iota(jnp.int32, (HALO, reach), 0) + HALO
    k_off = lax.broadcasted_iota(jnp.int32, (HALO, reach), 1)
    near = jnp.abs(q_off - k_off) <= RADIUS

    def light_tile(tile):
        at = tile * HALO
        key_pos = flat * rows + (at - HALO) + k_off
        allowed = near & (key_pos >= 0) & (key_pos < total_len)
        bias = jnp.where(allowed, 0.0, FLOOR)
        for head in range(lw // HDIM):
            lo_col, hi_col = head * HDIM, (head + 1) * HDIM
            light_mix[at : at + HALO, lo_col:hi_col] = softmax_mix(
                light_q[at : at + HALO, lo_col:hi_col],
                light_kv[at : at + reach, lo_col:hi_col],
                light_kv[at : at + reach, lw + lo_col : lw + hi_col],
                bias,
            )

    tiles = rows // HALO
    for tile in range(tiles):
        light_tile(tile)
        if tile == tiles // 2:
            send_query()
    forward_pair(0)
    loads[4].wait()

    query_core = []
    for i in range(len(spans)):
        query_x[i].wait_recv()
        query_core.append(join(*spans[i]))
        send_query()
        if i + 1 < len(pair_z):
            forward_pair(i + 1)
        if i >= 1:
            query_core[i - 1].wait_recv()
            start, size = spans[i - 1]
            queries[start - key_cap : start - key_cap + size] = (
                project(start, size, hq) * scale
            )
    for number in range(len(spans) + 1, len(pair_z)):
        forward_pair(number)
    wall_x = [remote(ho.at[part], walls.at[1, part], xp) for part in ours]
    for copy in wall_x:
        copy.start()
    query_core[-1].wait_recv()
    start, size = spans[-1]
    queries[start - key_cap : start - key_cap + size] = project(start, size, hq) * scale
    for copy in pair_y:
        copy.wait_recv()

    wall_y, wall_far = [], []

    def forward_wall():
        number = len(wall_y)
        if number < len(ours):
            wall_x[number].wait_recv()
            here = walls.at[1, ours[number]]
            wall_y.append(remote(here, here, yp))
            wall_y[-1].start()
            wall_far.append(remote(here, walls.at[2, ours[number]], core))
            wall_far[-1].start()

    keys = seq_count * key_cap
    step = TILE if keys <= 2048 else 32
    mix_x, mix_core, mix_far = [], [], []
    for i, (start, size) in enumerate(spans):
        at = start - key_cap

        def heavy_tile(tile, carry):
            here = pl.multiple_of(at + tile * step, step)
            for head in range(hw // HDIM):
                lo_col, hi_col = head * HDIM, (head + 1) * HDIM
                mix[0, pl.ds(here, step), lo_col:hi_col] = softmax_mix(
                    queries[pl.ds(here, step), lo_col:hi_col],
                    pairs[:, :, lo_col:hi_col].reshape(keys, HDIM),
                    pairs[:, :, hw + lo_col : hw + hi_col].reshape(keys, HDIM),
                    mask_ref[...],
                )
            return carry

        lax.fori_loop(0, size // step, heavy_tile, 0)
        here = pl.ds(at, size)
        mix_x.append(remote(mix.at[0, here], mix.at[2, here], xp))
        mix_x[-1].start()
        mix_core.append(remote(mix.at[0, here], mix.at[1, here], core))
        mix_core[-1].start()
        if i >= 1:
            mix_x[i - 1].wait_recv()
            before = pl.ds(at - TILE, TILE)
            mix_far.append(remote(mix.at[2, before], mix.at[3, before], core))
            mix_far[-1].start()
        if i >= len(spans) // 2 - 1:
            forward_wall()
    while len(wall_y) < len(ours):
        forward_wall()
    mix_x[-1].wait_recv()
    last = pl.ds(query_cap - TILE, TILE)
    mix_far.append(remote(mix.at[2, last], mix.at[3, last], core))
    mix_far[-1].start()

    def back(part):
        pick_t = chosen(key_cap, query_cap, h)
        placed[part] = lax.dot_general(
            pick_t, mix[part], (((0,), (0,)), ((), ())), preferred_element_type=jnp.float32
        ).astype(jnp.bfloat16)

    back(0)
    for copy in mix_core:
        copy.wait_recv()
    back(1)
    back(2)
    for copy in mix_far:
        copy.wait_recv()
    back(3)
    wall_core.wait_recv()
    for number, copy in enumerate(list(wall_y)):
        copy.wait_recv()
        here = walls.at[1, theirs[number]]
        wall_far.append(remote(here, walls.at[2, theirs[number]], core))
        wall_far[-1].start()
    for copy in wall_far:
        copy.wait_recv()
    loads[3].wait()

    def finish(tile, carry):
        here = pl.ds(pl.multiple_of(tile * TILE, TILE), TILE)
        out[here] = (
            dot32(light_mix[here], lo[...])
            + dot32(placed[0, here], ho[...])
            + dot32(placed[1, here], walls[0])
            + dot32(placed[2, here], walls[1])
            + dot32(placed[3, here], walls[2])
        ).astype(jnp.bfloat16)
        return carry

    lax.fori_loop(0, rows // TILE, finish, 0)

    waited = [key_x] + query_x[: len(query_x) - 2] + pair_z
    for copy in begun:
        if not any(copy is done for done in waited):
            copy.wait_send()


def shards(tokens, query_index, key_index, *weights):
    seq_count, group = lax.axis_size("seq"), lax.axis_size("head")
    rows, width = tokens.shape
    lw, hw = weights[0].shape[1], weights[4].shape[1]
    block_len = rows * group
    query_cap, key_cap = block_len // 4, 3 * block_len // 32
    slots = query_cap + key_cap
    copies = 8 + 2 * (seq_count // 2) + 5 * (query_cap // TILE) + 8
    bf16 = jnp.bfloat16
    return pl.pallas_call(
        functools.partial(kernel, seq_count, group),
        out_shape=jax.ShapeDtypeStruct(tokens.shape, bf16),
        in_specs=[pl.BlockSpec(memory_space=pltpu.VMEM)] * 3
        + [pl.BlockSpec(memory_space=pl.ANY)] * 8,
        out_specs=pl.BlockSpec(memory_space=pltpu.VMEM),
        scratch_shapes=[pltpu.VMEM(weight.shape, bf16) for weight in weights]
        + [
            pltpu.VMEM((rows, width // 2), bf16),
            pltpu.VMEM((slots, 1), jnp.int32),
            pltpu.VMEM((1, seq_count * key_cap), jnp.float32),
            pltpu.VMEM((slots, width // 2), bf16),
            pltpu.VMEM((slots, width // 2), bf16),
            pltpu.VMEM((slots, width // 2), bf16),
            pltpu.VMEM((rows, lw), bf16),
            pltpu.VMEM((rows + 2 * HALO, 2 * lw), bf16),
            pltpu.VMEM((rows, lw), bf16),
            pltpu.VMEM((seq_count, key_cap, 2 * hw), bf16),
            pltpu.VMEM((query_cap, hw), bf16),
            pltpu.VMEM((4, query_cap, hw), bf16),
            pltpu.VMEM((3,) + weights[7].shape, bf16),
            pltpu.VMEM((4, rows, hw), bf16),
            pltpu.SemaphoreType.DMA((8,)),
            pltpu.SemaphoreType.DMA((copies,)),
            pltpu.SemaphoreType.DMA((copies,)),
        ],
        compiler_params=pltpu.CompilerParams(
            collective_id=0, has_side_effects=True, vmem_limit_bytes=VMEM_LIMIT
        ),
    )(tokens, query_index.reshape(1, -1), key_index.reshape(1, -1), *weights)


def solution(mesh):
    placed = (
        P(("seq", "head"), None),
        P(),
        P(),
        P(),
        P(),
        P(),
        P(),
        P(None, "head"),
        P(None, "head"),
        P(None, "head"),
        P("head", None),
    )
    return jax.shard_map(
        shards, mesh=mesh, in_specs=placed, out_specs=P(("seq", "head"), None), check_vma=False
    )
```

```python
import functools

import jax
import jax.numpy as jnp
from jax import lax
from jax.experimental import pallas as pl
from jax.experimental.pallas import tpu as pltpu
from jax.sharding import PartitionSpec as P

HDIM = 64
RADIUS = 127
HALO = 128
TILE = 128
FLOOR = -1e30
VMEM_LIMIT = 60 * 1024 * 1024
MESH = pl.DeviceIdType.MESH


def dot32(a, b):
    return jnp.dot(a, b, preferred_element_type=jnp.float32)


def dot16(a, b):
    return dot32(a, b).astype(jnp.bfloat16)


def softmax_mix(q, k, v, bias):
    scores = lax.dot_general(
        q, k, (((1,), (1,)), ((), ())), preferred_element_type=jnp.float32
    ) + bias
    peak = jnp.max(scores, axis=1, keepdims=True)
    weights = jnp.exp(scores - peak)
    total = jnp.sum(weights, axis=1, keepdims=True)
    mixed = dot32(weights.astype(jnp.bfloat16), v)
    return (mixed / total).astype(jnp.bfloat16)


def slot_places(index_ref, cap, first_token):
    total = index_ref.shape[1]
    piece = min(total, 1024)
    before = jnp.zeros((1, 1), jnp.int32)
    for start in range(0, total, piece):
        part = index_ref[:, start : start + piece]
        before += jnp.sum((part < first_token).astype(jnp.int32), axis=1, keepdims=True)
    place = jnp.zeros((cap, 1), jnp.int32)
    for start in range(0, total, piece):
        part = index_ref[:, start : start + piece]
        rank = lax.broadcasted_iota(jnp.int32, (cap, piece), 1) + (start - before)
        slot = lax.broadcasted_iota(jnp.int32, (cap, piece), 0)
        place += jnp.sum(jnp.where(rank == slot, part + 1, 0), axis=1, keepdims=True)
    return place - 1 - first_token


def key_mask(index_ref, seq_count, cap, block_len):
    position = lax.broadcasted_iota(jnp.int32, (1, seq_count * cap), 1)
    index = index_ref[...]
    mask = jnp.zeros((1, seq_count * cap), jnp.int32)
    for block in range(seq_count):
        inside = (index >= block * block_len) & (index < (block + 1) * block_len)
        count = jnp.sum(inside.astype(jnp.int32), axis=1, keepdims=True)
        hit = (position >= block * cap) & (position < block * cap + count)
        mask = mask | hit.astype(jnp.int32)
    return jnp.where(mask > 0, 0.0, FLOOR)


def kernel(
    seq_count,
    group,
    tok,
    qi,
    ki,
    *refs,
):
    far, out, near_refs = refs[:8], refs[8], refs[9:17]
    lq, lk, lv, lo, hq, hk, hv, ho = near_refs
    (
        got_tok,
        place_ref,
        mask_ref,
        pick,
        pick_x,
        pick_core,
        light_q,
        light_kv,
        light_mix,
        pairs,
        queries,
        mix,
        walls,
        placed,
        load,
        send,
        recv,
    ) = refs[17:]
    loads = [
        pltpu.make_async_copy(a, b, load.at[i]) for i, (a, b) in enumerate(zip(far, near_refs))
    ]
    rows, width = tok.shape
    half = width // 2
    block_len = rows * group
    total_len = block_len * seq_count
    query_cap = queries.shape[0]
    key_cap = pairs.shape[1]
    hw = hq.shape[1]
    lw = lq.shape[1]
    zs = seq_count // 2
    s, h = lax.axis_index("seq"), lax.axis_index("head")
    x, c = h // 2, h % 2
    z, y = s // 2, s % 2
    core = (s, x * 2 + 1 - c)
    xp = (s, (1 - x) * 2 + c)
    yp = (z * 2 + 1 - y, h)
    zp = [None] + [(((z + d) % zs) * 2 + y, h) for d in range(1, zs)]
    flat, count = s * group + h, seq_count * group
    up, down = (flat + 1) % count, (flat + count - 1) % count
    above, below = (up // group, up % group), (down // group, down % group)
    partners = [core, xp, yp, above, below] + zp[1:]

    barrier = pltpu.get_barrier_semaphore()
    for device in partners:
        pl.semaphore_signal(barrier, inc=1, device_id=device, device_id_type=MESH)
    pl.semaphore_wait(barrier, len(partners))

    used = [0]
    begun = []

    def remote(src, dst, device):
        number = used[0]
        used[0] += 1
        copy = pltpu.make_async_remote_copy(
            src_ref=src,
            dst_ref=dst,
            send_sem=send.at[number],
            recv_sem=recv.at[number],
            device_id=device,
            device_id_type=MESH,
        )
        begun.append(copy)
        return copy

    mine = pl.multiple_of(c * half, half)
    other = pl.multiple_of((1 - c) * half, half)
    tok_copy = remote(tok.at[:, pl.ds(other, half)], got_tok, core)
    tok_copy.start()
    zl = z % 2
    zmate = ((z + 1 - 2 * zl) * 2 + y, h)
    piece = ho.shape[0] // 4
    first_piece = pl.ds(pl.multiple_of((zl * 2 + y) * piece, piece), piece)
    first_half = pl.ds(pl.multiple_of(zl * 2 * piece, 2 * piece), 2 * piece)
    rest_half = pl.ds(pl.multiple_of((1 - zl) * 2 * piece, 2 * piece), 2 * piece)
    wall_x = remote(far[7].at[first_piece], walls.at[1, first_piece], xp)
    wall_x.start()
    for i in (0, 1, 2, 5, 6, 4, 7, 3):
        loads[i].start()

    first_token = s * block_len
    place_ref[:key_cap] = slot_places(ki, key_cap, first_token)
    place_ref[key_cap:] = slot_places(qi, query_cap, first_token)
    mask_ref[...] = key_mask(ki, seq_count, key_cap, block_len)

    def chosen(start, size, owner):
        ids = lax.broadcasted_iota(jnp.int32, (size, rows), 1) + owner * rows
        hit = place_ref[start : start + size] == ids
        return hit.astype(jnp.float32).astype(jnp.bfloat16)

    def choose(start, size):
        pick[start : start + size] = (
            dot32(chosen(start, size, h), tok[:, pl.ds(mine, half)])
            + dot32(chosen(start, size, core[1]), got_tok[...])
        ).astype(jnp.bfloat16)

    tok_copy.wait_recv()
    choose(0, key_cap)
    span = pl.ds(0, key_cap)
    key_x = remote(pick.at[span], pick_x.at[span], xp)
    key_x.start()

    spans = [(key_cap + i * TILE, TILE) for i in range(query_cap // TILE)]
    for start, size in spans:
        choose(start, size)

    scale = jnp.asarray(HDIM**-0.5, jnp.bfloat16)
    for i in (0, 1, 2):
        loads[i].wait()

    def light_project(tile, carry):
        at = pl.multiple_of(tile * TILE, TILE)
        part = tok[pl.ds(at, TILE)]
        light_q[pl.ds(at, TILE)] = (dot32(part, lq[...]).astype(jnp.bfloat16)) * scale
        light_kv[pl.ds(at + HALO, TILE), :lw] = dot16(part, lk[...])
        light_kv[pl.ds(at + HALO, TILE), lw:] = dot16(part, lv[...])
        return carry

    lax.fori_loop(0, rows // TILE, light_project, 0)
    to_above = remote(light_kv.at[pl.ds(rows, HALO)], light_kv.at[pl.ds(0, HALO)], above)
    to_above.start()
    to_below = remote(
        light_kv.at[pl.ds(HALO, HALO)], light_kv.at[pl.ds(rows + HALO, HALO)], below
    )
    to_below.start()

    key_x.wait()
    wall_x.wait_recv()
    wall_y = remote(walls.at[1, first_piece], walls.at[1, first_piece], yp)
    wall_y.start()

    def join(start, size):
        rows_here = pl.ds(start, size)
        pick_x[rows_here] = pick[rows_here] + pick_x[rows_here]
        copy = remote(pick_x.at[rows_here], pick_core.at[rows_here], core)
        copy.start()
        return copy

    def project(start, size, matrix):
        return (
            dot32(pick_x[start : start + size], matrix[pl.ds(mine, half)])
            + dot32(pick_core[start : start + size], matrix[pl.ds(other, half)])
        ).astype(jnp.bfloat16)

    query_x = [
        remote(pick.at[pl.ds(start, size)], pick_x.at[pl.ds(start, size)], xp)
        for start, size in spans
    ]
    sent = [0]

    def send_query():
        if sent[0] < len(query_x):
            if sent[0] >= 2:
                query_x[sent[0] - 2].wait_send()
            query_x[sent[0]].start()
            sent[0] += 1

    key_core = join(0, key_cap)
    send_query()
    send_query()
    loads[5].wait()
    loads[6].wait()
    key_core.wait_recv()
    pairs[s, :, :hw] = project(0, key_cap, hk)
    pairs[s, :, hw:] = project(0, key_cap, hv)
    order = sorted(range(1, zs), key=lambda d: min(d, zs - d))
    pair_z = [remote(pairs.at[s], pairs.at[s], zp[d]) for d in order]
    pair_z[0].start()
    pair_y = [remote(pairs.at[s], pairs.at[s], yp)]
    pair_y[0].start()
    loads[7].wait()
    wall_core = remote(ho, walls.at[0], core)
    wall_core.start()
    wall_y.wait_recv()
    wall_far_a = remote(walls.at[1, first_half], walls.at[2, first_half], core)
    wall_far_a.start()

    def forward_pair(number):
        pair_z[number].wait()
        if number + 1 < len(pair_z):
            pair_z[number + 1].start()
        slot = ((z + zs - order[number]) % zs) * 2 + y
        copy = remote(pairs.at[slot], pairs.at[slot], yp)
        copy.start()
        pair_y.append(copy)

    to_above.wait_recv()
    to_below.wait_recv()
    reach = 3 * HALO
    q_off = lax.broadcasted_iota(jnp.int32, (HALO, reach), 0) + HALO
    k_off = lax.broadcasted_iota(jnp.int32, (HALO, reach), 1)
    near = jnp.abs(q_off - k_off) <= RADIUS

    def light_tile(tile):
        at = tile * HALO
        key_pos = flat * rows + (at - HALO) + k_off
        allowed = near & (key_pos >= 0) & (key_pos < total_len)
        bias = jnp.where(allowed, 0.0, FLOOR)
        for head in range(lw // HDIM):
            lo_col, hi_col = head * HDIM, (head + 1) * HDIM
            light_mix[at : at + HALO, lo_col:hi_col] = softmax_mix(
                light_q[at : at + HALO, lo_col:hi_col],
                light_kv[at : at + reach, lo_col:hi_col],
                light_kv[at : at + reach, lw + lo_col : lw + hi_col],
                bias,
            )

    tiles = rows // HALO
    for tile in range(tiles):
        light_tile(tile)
        if tile == tiles // 2:
            send_query()
    forward_pair(0)
    loads[4].wait()

    query_core = []
    for i in range(len(spans)):
        query_x[i].wait_recv()
        query_core.append(join(*spans[i]))
        send_query()
        if i + 1 < len(pair_z):
            forward_pair(i + 1)
        if i >= 1:
            query_core[i - 1].wait_recv()
            start, size = spans[i - 1]
            queries[start - key_cap : start - key_cap + size] = (
                project(start, size, hq) * scale
            )
    for number in range(len(spans) + 1, len(pair_z)):
        forward_pair(number)
    wall_z = remote(walls.at[1, first_half], walls.at[1, first_half], zmate)
    wall_z.start()
    query_core[-1].wait_recv()
    start, size = spans[-1]
    queries[start - key_cap : start - key_cap + size] = project(start, size, hq) * scale
    for copy in pair_y:
        copy.wait_recv()

    keys = seq_count * key_cap
    step = TILE if keys <= 2048 else 32
    mix_x, mix_core, mix_far = [], [], []
    for i, (start, size) in enumerate(spans):
        at = start - key_cap

        def heavy_tile(tile, carry):
            here = pl.multiple_of(at + tile * step, step)
            for head in range(hw // HDIM):
                lo_col, hi_col = head * HDIM, (head + 1) * HDIM
                mix[0, pl.ds(here, step), lo_col:hi_col] = softmax_mix(
                    queries[pl.ds(here, step), lo_col:hi_col],
                    pairs[:, :, lo_col:hi_col].reshape(keys, HDIM),
                    pairs[:, :, hw + lo_col : hw + hi_col].reshape(keys, HDIM),
                    mask_ref[...],
                )
            return carry

        lax.fori_loop(0, size // step, heavy_tile, 0)
        here = pl.ds(at, size)
        mix_x.append(remote(mix.at[0, here], mix.at[2, here], xp))
        mix_x[-1].start()
        mix_core.append(remote(mix.at[0, here], mix.at[1, here], core))
        mix_core[-1].start()
        if i >= 1:
            mix_x[i - 1].wait_recv()
            before = pl.ds(at - TILE, TILE)
            mix_far.append(remote(mix.at[2, before], mix.at[3, before], core))
            mix_far[-1].start()
    mix_x[-1].wait_recv()
    last = pl.ds(query_cap - TILE, TILE)
    mix_far.append(remote(mix.at[2, last], mix.at[3, last], core))
    mix_far[-1].start()

    def back(part):
        pick_t = chosen(key_cap, query_cap, h)
        placed[part] = lax.dot_general(
            pick_t, mix[part], (((0,), (0,)), ((), ())), preferred_element_type=jnp.float32
        ).astype(jnp.bfloat16)

    back(0)
    for copy in mix_core:
        copy.wait_recv()
    back(1)
    back(2)
    for copy in mix_far:
        copy.wait_recv()
    back(3)
    wall_core.wait_recv()
    wall_far_a.wait_recv()
    wall_z.wait_recv()
    wall_far_b = remote(walls.at[1, rest_half], walls.at[2, rest_half], core)
    wall_far_b.start()
    wall_far_b.wait_recv()
    loads[3].wait()

    def finish(tile, carry):
        here = pl.ds(pl.multiple_of(tile * TILE, TILE), TILE)
        out[here] = (
            dot32(light_mix[here], lo[...])
            + dot32(placed[0, here], ho[...])
            + dot32(placed[1, here], walls[0])
            + dot32(placed[2, here], walls[1])
            + dot32(placed[3, here], walls[2])
        ).astype(jnp.bfloat16)
        return carry

    lax.fori_loop(0, rows // TILE, finish, 0)

    waited = [key_x] + query_x[: len(query_x) - 2] + pair_z
    for copy in begun:
        if not any(copy is done for done in waited):
            copy.wait_send()


def shards(tokens, query_index, key_index, *weights):
    seq_count, group = lax.axis_size("seq"), lax.axis_size("head")
    rows, width = tokens.shape
    lw, hw = weights[0].shape[1], weights[4].shape[1]
    block_len = rows * group
    query_cap, key_cap = block_len // 4, 3 * block_len // 32
    slots = query_cap + key_cap
    copies = 8 + 2 * (seq_count // 2) + 5 * (query_cap // TILE) + 8
    bf16 = jnp.bfloat16
    return pl.pallas_call(
        functools.partial(kernel, seq_count, group),
        out_shape=jax.ShapeDtypeStruct(tokens.shape, bf16),
        in_specs=[pl.BlockSpec(memory_space=pltpu.VMEM)] * 3
        + [pl.BlockSpec(memory_space=pl.ANY)] * 8,
        out_specs=pl.BlockSpec(memory_space=pltpu.VMEM),
        scratch_shapes=[pltpu.VMEM(weight.shape, bf16) for weight in weights]
        + [
            pltpu.VMEM((rows, width // 2), bf16),
            pltpu.VMEM((slots, 1), jnp.int32),
            pltpu.VMEM((1, seq_count * key_cap), jnp.float32),
            pltpu.VMEM((slots, width // 2), bf16),
            pltpu.VMEM((slots, width // 2), bf16),
            pltpu.VMEM((slots, width // 2), bf16),
            pltpu.VMEM((rows, lw), bf16),
            pltpu.VMEM((rows + 2 * HALO, 2 * lw), bf16),
            pltpu.VMEM((rows, lw), bf16),
            pltpu.VMEM((seq_count, key_cap, 2 * hw), bf16),
            pltpu.VMEM((query_cap, hw), bf16),
            pltpu.VMEM((4, query_cap, hw), bf16),
            pltpu.VMEM((3,) + weights[7].shape, bf16),
            pltpu.VMEM((4, rows, hw), bf16),
            pltpu.SemaphoreType.DMA((8,)),
            pltpu.SemaphoreType.DMA((copies,)),
            pltpu.SemaphoreType.DMA((copies,)),
        ],
        compiler_params=pltpu.CompilerParams(
            collective_id=0, has_side_effects=True, vmem_limit_bytes=VMEM_LIMIT
        ),
    )(tokens, query_index.reshape(1, -1), key_index.reshape(1, -1), *weights)


def solution(mesh):
    placed = (
        P(("seq", "head"), None),
        P(),
        P(),
        P(),
        P(),
        P(),
        P(),
        P(None, "head"),
        P(None, "head"),
        P(None, "head"),
        P("head", None),
    )
    return jax.shard_map(
        shards, mesh=mesh, in_specs=placed, out_specs=P(("seq", "head"), None), check_vma=False
    )
```

```python
import functools

import jax
import jax.numpy as jnp
from jax import lax
from jax.experimental import pallas as pl
from jax.experimental.pallas import tpu as pltpu
from jax.sharding import PartitionSpec as P

HDIM = 64
RADIUS = 127
HALO = 128
TILE = 128
FLOOR = -1e30
VMEM_LIMIT = 60 * 1024 * 1024
MESH = pl.DeviceIdType.MESH


def dot32(a, b):
    return jnp.dot(a, b, preferred_element_type=jnp.float32)


def dot16(a, b):
    return dot32(a, b).astype(jnp.bfloat16)


def softmax_mix(q, k, v, bias):
    scores = lax.dot_general(
        q, k, (((1,), (1,)), ((), ())), preferred_element_type=jnp.float32
    ) + bias
    peak = jnp.max(scores, axis=1, keepdims=True)
    weights = jnp.exp(scores - peak)
    total = jnp.sum(weights, axis=1, keepdims=True)
    mixed = dot32(weights.astype(jnp.bfloat16), v)
    return (mixed / total).astype(jnp.bfloat16)


def slot_places(index_ref, cap, first_token):
    total = index_ref.shape[1]
    piece = min(total, 1024)
    before = jnp.zeros((1, 1), jnp.int32)
    for start in range(0, total, piece):
        part = index_ref[:, start : start + piece]
        before += jnp.sum((part < first_token).astype(jnp.int32), axis=1, keepdims=True)
    place = jnp.zeros((cap, 1), jnp.int32)
    for start in range(0, total, piece):
        part = index_ref[:, start : start + piece]
        rank = lax.broadcasted_iota(jnp.int32, (cap, piece), 1) + (start - before)
        slot = lax.broadcasted_iota(jnp.int32, (cap, piece), 0)
        place += jnp.sum(jnp.where(rank == slot, part + 1, 0), axis=1, keepdims=True)
    return place - 1 - first_token


def key_mask(index_ref, seq_count, cap, block_len):
    position = lax.broadcasted_iota(jnp.int32, (1, seq_count * cap), 1)
    index = index_ref[...]
    mask = jnp.zeros((1, seq_count * cap), jnp.int32)
    for block in range(seq_count):
        inside = (index >= block * block_len) & (index < (block + 1) * block_len)
        count = jnp.sum(inside.astype(jnp.int32), axis=1, keepdims=True)
        hit = (position >= block * cap) & (position < block * cap + count)
        mask = mask | hit.astype(jnp.int32)
    return jnp.where(mask > 0, 0.0, FLOOR)


def kernel(
    seq_count,
    group,
    tok,
    qi,
    ki,
    *refs,
):
    far, out, near_refs = refs[:8], refs[8], refs[9:17]
    lq, lk, lv, lo, hq, hk, hv, ho = near_refs
    (
        got_tok,
        place_ref,
        mask_ref,
        pick,
        pick_x,
        pick_core,
        light_q,
        light_kv,
        light_mix,
        pairs,
        queries,
        mix,
        walls,
        placed,
        back_ref,
        load,
        send,
        recv,
    ) = refs[17:]
    loads = [
        pltpu.make_async_copy(a, b, load.at[i]) for i, (a, b) in enumerate(zip(far, near_refs))
    ]
    rows, width = tok.shape
    half = width // 2
    block_len = rows * group
    total_len = block_len * seq_count
    query_cap = queries.shape[0]
    key_cap = pairs.shape[1]
    hw = hq.shape[1]
    lw = lq.shape[1]
    zs = seq_count // 2
    s, h = lax.axis_index("seq"), lax.axis_index("head")
    x, c = h // 2, h % 2
    z, y = s // 2, s % 2
    core = (s, x * 2 + 1 - c)
    xp = (s, (1 - x) * 2 + c)
    yp = (z * 2 + 1 - y, h)
    zp = [None] + [(((z + d) % zs) * 2 + y, h) for d in range(1, zs)]
    flat, count = s * group + h, seq_count * group
    up, down = (flat + 1) % count, (flat + count - 1) % count
    above, below = (up // group, up % group), (down // group, down % group)
    partners = [core, xp, yp, above, below] + zp[1:]

    barrier = pltpu.get_barrier_semaphore()
    for device in partners:
        pl.semaphore_signal(barrier, inc=1, device_id=device, device_id_type=MESH)
    pl.semaphore_wait(barrier, len(partners))

    used = [0]
    begun = []

    def remote(src, dst, device):
        number = used[0]
        used[0] += 1
        copy = pltpu.make_async_remote_copy(
            src_ref=src,
            dst_ref=dst,
            send_sem=send.at[number],
            recv_sem=recv.at[number],
            device_id=device,
            device_id_type=MESH,
        )
        begun.append(copy)
        return copy

    mine = pl.multiple_of(c * half, half)
    other = pl.multiple_of((1 - c) * half, half)
    tok_copy = remote(tok.at[:, pl.ds(other, half)], got_tok, core)
    tok_copy.start()
    zl = z % 2
    zmate = ((z + 1 - 2 * zl) * 2 + y, h)
    piece = ho.shape[0] // 4
    first_piece = pl.ds(pl.multiple_of((zl * 2 + y) * piece, piece), piece)
    first_half = pl.ds(pl.multiple_of(zl * 2 * piece, 2 * piece), 2 * piece)
    rest_half = pl.ds(pl.multiple_of((1 - zl) * 2 * piece, 2 * piece), 2 * piece)
    wall_x = remote(far[7].at[first_piece], walls.at[1, first_piece], xp)
    wall_x.start()
    for i in (0, 1, 2, 5, 6, 4, 7, 3):
        loads[i].start()

    first_token = s * block_len
    place_ref[:key_cap] = slot_places(ki, key_cap, first_token)
    place_ref[key_cap:] = slot_places(qi, query_cap, first_token)
    mask_ref[...] = key_mask(ki, seq_count, key_cap, block_len)

    def chosen(start, size, owner):
        ids = lax.broadcasted_iota(jnp.int32, (size, rows), 1) + owner * rows
        hit = place_ref[start : start + size] == ids
        return hit.astype(jnp.float32).astype(jnp.bfloat16)

    def choose(start, size):
        pick[start : start + size] = (
            dot32(chosen(start, size, h), tok[:, pl.ds(mine, half)])
            + dot32(chosen(start, size, core[1]), got_tok[...])
        ).astype(jnp.bfloat16)

    tok_copy.wait_recv()
    choose(0, key_cap)
    span = pl.ds(0, key_cap)
    key_x = remote(pick.at[span], pick_x.at[span], xp)
    key_x.start()

    spans = [(key_cap + i * TILE, TILE) for i in range(query_cap // TILE)]
    for start, size in spans:
        choose(start, size)

    scale = jnp.asarray(HDIM**-0.5, jnp.bfloat16)
    for i in (0, 1, 2):
        loads[i].wait()

    def light_project(tile, carry):
        at = pl.multiple_of(tile * TILE, TILE)
        part = tok[pl.ds(at, TILE)]
        light_q[pl.ds(at, TILE)] = (dot32(part, lq[...]).astype(jnp.bfloat16)) * scale
        light_kv[pl.ds(at + HALO, TILE), :lw] = dot16(part, lk[...])
        light_kv[pl.ds(at + HALO, TILE), lw:] = dot16(part, lv[...])
        return carry

    lax.fori_loop(0, rows // TILE, light_project, 0)
    to_above = remote(light_kv.at[pl.ds(rows, HALO)], light_kv.at[pl.ds(0, HALO)], above)
    to_above.start()
    to_below = remote(
        light_kv.at[pl.ds(HALO, HALO)], light_kv.at[pl.ds(rows + HALO, HALO)], below
    )
    to_below.start()

    key_x.wait()
    wall_x.wait_recv()
    wall_y = remote(walls.at[1, first_piece], walls.at[1, first_piece], yp)
    wall_y.start()

    def join(start, size):
        rows_here = pl.ds(start, size)
        pick_x[rows_here] = pick[rows_here] + pick_x[rows_here]
        copy = remote(pick_x.at[rows_here], pick_core.at[rows_here], core)
        copy.start()
        return copy

    def project(start, size, matrix):
        return (
            dot32(pick_x[start : start + size], matrix[pl.ds(mine, half)])
            + dot32(pick_core[start : start + size], matrix[pl.ds(other, half)])
        ).astype(jnp.bfloat16)

    query_x = [
        remote(pick.at[pl.ds(start, size)], pick_x.at[pl.ds(start, size)], xp)
        for start, size in spans
    ]
    sent = [0]

    def send_query():
        if sent[0] < len(query_x):
            if sent[0] >= 2:
                query_x[sent[0] - 2].wait_send()
            query_x[sent[0]].start()
            sent[0] += 1

    key_core = join(0, key_cap)
    send_query()
    send_query()
    loads[5].wait()
    loads[6].wait()
    key_core.wait_recv()
    pairs[s, :, :hw] = project(0, key_cap, hk)
    pairs[s, :, hw:] = project(0, key_cap, hv)
    order = sorted(range(1, zs), key=lambda d: min(d, zs - d))
    pair_z = [remote(pairs.at[s], pairs.at[s], zp[d]) for d in order]
    pair_z[0].start()
    pair_y = [remote(pairs.at[s], pairs.at[s], yp)]
    pair_y[0].start()
    loads[7].wait()
    wall_core = remote(ho, walls.at[0], core)
    wall_core.start()
    wall_y.wait_recv()
    wall_far_a = remote(walls.at[1, first_half], walls.at[2, first_half], core)
    wall_far_a.start()

    def forward_pair(number):
        pair_z[number].wait()
        if number + 1 < len(pair_z):
            pair_z[number + 1].start()
        slot = ((z + zs - order[number]) % zs) * 2 + y
        copy = remote(pairs.at[slot], pairs.at[slot], yp)
        copy.start()
        pair_y.append(copy)

    to_above.wait_recv()
    to_below.wait_recv()
    reach = 3 * HALO
    q_off = lax.broadcasted_iota(jnp.int32, (HALO, reach), 0) + HALO
    k_off = lax.broadcasted_iota(jnp.int32, (HALO, reach), 1)
    near = jnp.abs(q_off - k_off) <= RADIUS

    def light_tile(tile):
        at = tile * HALO
        key_pos = flat * rows + (at - HALO) + k_off
        allowed = near & (key_pos >= 0) & (key_pos < total_len)
        bias = jnp.where(allowed, 0.0, FLOOR)
        for head in range(lw // HDIM):
            lo_col, hi_col = head * HDIM, (head + 1) * HDIM
            light_mix[at : at + HALO, lo_col:hi_col] = softmax_mix(
                light_q[at : at + HALO, lo_col:hi_col],
                light_kv[at : at + reach, lo_col:hi_col],
                light_kv[at : at + reach, lw + lo_col : lw + hi_col],
                bias,
            )

    tiles = rows // HALO
    for tile in range(tiles):
        light_tile(tile)
        if tile == tiles // 2:
            send_query()
    forward_pair(0)
    loads[4].wait()

    query_core = []
    for i in range(len(spans) - 1):
        query_x[i].wait_recv()
        query_core.append(join(*spans[i]))
        send_query()
        if i + 1 < len(pair_z):
            forward_pair(i + 1)
        if i >= 1:
            query_core[i - 1].wait_recv()
            start, size = spans[i - 1]
            queries[start - key_cap : start - key_cap + size] = (
                project(start, size, hq) * scale
            )
    for number in range(len(spans), len(pair_z)):
        forward_pair(number)
    wall_z = remote(walls.at[1, first_half], walls.at[1, first_half], zmate)
    wall_z.start()
    while sent[0] < len(query_x):
        send_query()

    def settle(i):
        query_core[i].wait_recv()
        start, size = spans[i]
        queries[start - key_cap : start - key_cap + size] = project(start, size, hq) * scale

    settle(len(spans) - 2)
    back_ref[...] = (
        chosen(key_cap, query_cap, h).astype(jnp.float32).T.astype(jnp.bfloat16)
    )
    for copy in pair_y:
        copy.wait_recv()

    keys = seq_count * key_cap
    step = TILE if keys <= 2048 else 32
    mix_x, mix_core, mix_far = [], [], []
    for i, (start, size) in enumerate(spans):
        at = start - key_cap
        if i == len(spans) - 2:
            query_x[-1].wait_recv()
            query_core.append(join(*spans[-1]))
        if i == len(spans) - 1:
            settle(i)

        def heavy_tile(tile, carry):
            here = pl.multiple_of(at + tile * step, step)
            for head in range(hw // HDIM):
                lo_col, hi_col = head * HDIM, (head + 1) * HDIM
                mix[0, pl.ds(here, step), lo_col:hi_col] = softmax_mix(
                    queries[pl.ds(here, step), lo_col:hi_col],
                    pairs[:, :, lo_col:hi_col].reshape(keys, HDIM),
                    pairs[:, :, hw + lo_col : hw + hi_col].reshape(keys, HDIM),
                    mask_ref[...],
                )
            return carry

        lax.fori_loop(0, size // step, heavy_tile, 0)
        here = pl.ds(at, size)
        mix_x.append(remote(mix.at[0, here], mix.at[2, here], xp))
        mix_x[-1].start()
        mix_core.append(remote(mix.at[0, here], mix.at[1, here], core))
        mix_core[-1].start()
        if i >= 1:
            mix_x[i - 1].wait_recv()
            before = pl.ds(at - TILE, TILE)
            mix_far.append(remote(mix.at[2, before], mix.at[3, before], core))
            mix_far[-1].start()
    mix_x[-1].wait_recv()
    last = pl.ds(query_cap - TILE, TILE)
    mix_far.append(remote(mix.at[2, last], mix.at[3, last], core))
    mix_far[-1].start()

    wall_far_a.wait_recv()
    wall_z.wait_recv()
    wall_far_b = remote(walls.at[1, rest_half], walls.at[2, rest_half], core)
    wall_far_b.start()

    def back(part):
        placed[part] = dot16(back_ref[...], mix[part])

    back(0)
    for copy in mix_core:
        copy.wait_recv()
    back(1)
    back(2)
    for copy in mix_far:
        copy.wait_recv()
    back(3)
    wall_core.wait_recv()
    wall_far_b.wait_recv()
    loads[3].wait()

    def finish(tile, carry):
        here = pl.ds(pl.multiple_of(tile * TILE, TILE), TILE)
        out[here] = (
            dot32(light_mix[here], lo[...])
            + dot32(placed[0, here], ho[...])
            + dot32(placed[1, here], walls[0])
            + dot32(placed[2, here], walls[1])
            + dot32(placed[3, here], walls[2])
        ).astype(jnp.bfloat16)
        return carry

    lax.fori_loop(0, rows // TILE, finish, 0)

    waited = [key_x] + query_x[: len(query_x) - 2] + pair_z
    for copy in begun:
        if not any(copy is done for done in waited):
            copy.wait_send()


def shards(tokens, query_index, key_index, *weights):
    seq_count, group = lax.axis_size("seq"), lax.axis_size("head")
    rows, width = tokens.shape
    lw, hw = weights[0].shape[1], weights[4].shape[1]
    block_len = rows * group
    query_cap, key_cap = block_len // 4, 3 * block_len // 32
    slots = query_cap + key_cap
    copies = 8 + 2 * (seq_count // 2) + 5 * (query_cap // TILE) + 8
    bf16 = jnp.bfloat16
    return pl.pallas_call(
        functools.partial(kernel, seq_count, group),
        out_shape=jax.ShapeDtypeStruct(tokens.shape, bf16),
        in_specs=[pl.BlockSpec(memory_space=pltpu.VMEM)] * 3
        + [pl.BlockSpec(memory_space=pl.ANY)] * 8,
        out_specs=pl.BlockSpec(memory_space=pltpu.VMEM),
        scratch_shapes=[pltpu.VMEM(weight.shape, bf16) for weight in weights]
        + [
            pltpu.VMEM((rows, width // 2), bf16),
            pltpu.VMEM((slots, 1), jnp.int32),
            pltpu.VMEM((1, seq_count * key_cap), jnp.float32),
            pltpu.VMEM((slots, width // 2), bf16),
            pltpu.VMEM((slots, width // 2), bf16),
            pltpu.VMEM((slots, width // 2), bf16),
            pltpu.VMEM((rows, lw), bf16),
            pltpu.VMEM((rows + 2 * HALO, 2 * lw), bf16),
            pltpu.VMEM((rows, lw), bf16),
            pltpu.VMEM((seq_count, key_cap, 2 * hw), bf16),
            pltpu.VMEM((query_cap, hw), bf16),
            pltpu.VMEM((4, query_cap, hw), bf16),
            pltpu.VMEM((3,) + weights[7].shape, bf16),
            pltpu.VMEM((4, rows, hw), bf16),
            pltpu.VMEM((rows, query_cap), bf16),
            pltpu.SemaphoreType.DMA((8,)),
            pltpu.SemaphoreType.DMA((copies,)),
            pltpu.SemaphoreType.DMA((copies,)),
        ],
        compiler_params=pltpu.CompilerParams(
            collective_id=0, has_side_effects=True, vmem_limit_bytes=VMEM_LIMIT
        ),
    )(tokens, query_index.reshape(1, -1), key_index.reshape(1, -1), *weights)


def solution(mesh):
    placed = (
        P(("seq", "head"), None),
        P(),
        P(),
        P(),
        P(),
        P(),
        P(),
        P(None, "head"),
        P(None, "head"),
        P(None, "head"),
        P("head", None),
    )
    return jax.shard_map(
        shards, mesh=mesh, in_specs=placed, out_specs=P(("seq", "head"), None), check_vma=False
    )
```
